32 devices in a mesh: pole: 2 (over y), row: 4 (over z), col: 4 (over x, core).
Axes of the slice: x: 2, y: 2, z: 4, core: 2. Of those that a mesh axis runs over, the one named last changes fastest.
Arguments:
- ancestors: bfloat16 [4096, 2048], P(('pole', 'row'), 'col'), parts along dimension 0, may hold values from -6 to 6
- panel: bfloat16 [4, 4096, 256], P(None, ('pole', 'row')), parts along dimension 1, may hold values from -0.125 to 0.125
- coupling: bfloat16 [6, 256, 256], P('pole'), parts along dimension 0, may hold values from -0.375 to 0.375
- pivots: bfloat16 [8, 256, 256], P('pole'), parts along dimension 0, may hold values from -6 to 6
- tile_lists: int32 [4, 8], replicated, may hold values from 0 to 8, as said below
Outputs:
- columns: float32 [4, 4096, 256], P(None, ('pole', 'row', 'col')), parts along dimension 1
- diagonal_blocks: float32 [8, 256, 256], P('pole', 'col'), parts along dimension 0
- linking_blocks: float32 [6, 256, 256], P('pole', 'col'), parts along dimension 0
The draws below stay inside these ranges and needn't reach their ends.
There are 2 independent parts, one for each index of `pole`. The reference program is written for one: setup_inputs(seed, part) draws one part's arguments, and reference() takes and returns one part's arrays. A program takes and returns all parts, laid end to end along the dimension named above; an argument that names none is the same for every part. Nothing has to cross between parts.
Inputs may be any that keep to these rules, and one draw needn't show every extreme that they name: `tile_lists`: each row lists distinct tiles of the region first, then is padded with 8; the tiles of row s + 1 are among those of row s, and row 0 names every tile; each row names at least half of the tiles.
All inputs are finite; a program needn't handle non-finite values.
Results may differ from the reference program's by a relative error of at most 0.0003.
Values may be sent and summed in bfloat16 or wider, within the bound.
A program may use at most 64 MiB of HBM per device.

```python
import jax
import jax.numpy as jnp
from jax import lax

B = 256
NSUP = 4
NB = 8
R = 2048


def draw_tile_lists(key, part):
    key = jax.random.fold_in(key, 7)
    key_order, key_count = jax.random.split(key)
    tile_order = jax.random.permutation(key_order, NB).astype(jnp.int32)
    removed = jax.random.randint(key_count, (NSUP,), 1, max(NB // (2 * NSUP), 1) + 1).astype(jnp.int32)
    removed = jnp.where(jnp.arange(NSUP) == 0, 0, removed).astype(jnp.int32)
    counts = (NB - jnp.cumsum(removed)).astype(jnp.int32)
    positions = jnp.arange(NB, dtype=jnp.int32)
    return jnp.where(positions[None, :] < counts[:, None], tile_order[None, :], NB).astype(jnp.int32)


def block_levels(rng, extent, cuts, least, high):
    level = 1.0
    for dim, blocks in cuts:
        draws = jax.random.uniform(jax.random.fold_in(jax.random.fold_in(rng, 6), dim), (blocks,), jnp.float32, least / len(cuts), high / len(cuts))
        level = level * jnp.repeat(jnp.exp(draws), extent[dim] // blocks).reshape((-1,) + (1,) * (len(extent) - 1 - dim))
    return level


def noise(stream_key, shape, deviation, most, pieces=(), held_as=jnp.bfloat16):
    entries = deviation * jax.random.normal(stream_key, shape, jnp.float32)
    if pieces:
        entries = entries * block_levels(stream_key, shape, pieces, -0.22, 0.18)
    return jnp.clip(entries, -most, most).astype(held_as)


def setup_inputs(seed: int = 0, part: int = 0) -> dict:
    arg_keys = jax.random.split(jax.random.key(seed), 6)
    part_splits = jax.random.split(jax.random.fold_in(arg_keys[5], part), 6)
    return {
        "ancestors": noise(part_splits[0], (R, R), 1.0, 6.0, ((0, 4), (1, 4))),
        "panel": noise(part_splits[1], (NSUP, R, B), R ** -0.5, 0.125, ((1, 4),)),
        "coupling": noise(part_splits[2], (NSUP - 1, B, B), B ** -0.5, 0.375),
        "pivots": noise(part_splits[3], (NSUP, B, B), 1.0, 6.0),
        "tile_lists": draw_tile_lists(jax.random.fold_in(arg_keys[5], 71), part),
    }


def reference(ancestors, panel, coupling, pivots, tile_lists):
    tile_ids = (jnp.arange(R, dtype=jnp.int32) // B).astype(jnp.int32)
    member = jnp.any(tile_lists[:, :, None] == tile_ids[None, None, :], axis=1)
    masked = jnp.where(member[:, :, None], panel, jnp.zeros((), panel.dtype))
    highest = lax.Precision.HIGHEST
    columns = []
    diagonals = []
    linking = []
    previous = None
    for sup_idx in range(NSUP):
        image_rows = jnp.dot(ancestors, masked[sup_idx], preferred_element_type=jnp.float32)
        link_f = None
        if sup_idx > 0:
            link_f = coupling[sup_idx - 1].astype(jnp.float32)
            image_rows = image_rows + jnp.dot(previous, link_f, precision=highest)
        column_out = jnp.where(member[sup_idx][:, None], -image_rows, jnp.float32(0.0))
        piece_f = masked[sup_idx].astype(jnp.float32)
        gram = jnp.dot(piece_f.T, column_out, precision=highest)
        pivot_f = pivots[sup_idx].astype(jnp.float32)
        if sup_idx > 0:
            cross = jnp.dot(previous.T, piece_f, precision=highest)
            linked = -(cross + jnp.dot(diagonals[-1], link_f, precision=highest))
            linking.append(linked)
            diagonals.append(pivot_f - gram - jnp.dot(link_f.T, linked, precision=highest))
        else:
            diagonals.append(pivot_f - gram)
        columns.append(column_out)
        previous = column_out
    return jnp.stack(columns), jnp.stack(diagonals), jnp.stack(linking)
```

```python
import functools

import jax
import jax.numpy as jnp
from jax import lax
from jax.experimental import pallas as pl
from jax.experimental.pallas import tpu as pltpu
from jax.sharding import PartitionSpec as P

F32 = jnp.float32
BF16 = jnp.bfloat16
MESH = pl.DeviceIdType.MESH
CORES = 2


def dot(a, b):
    return lax.dot_general(a, b, (((1,), (0,)), ((), ())), preferred_element_type=F32)


def dot_t(a, b):
    return lax.dot_general(a, b, (((0,), (0,)), ((), ())), preferred_element_type=F32)


def split(x):
    hi = x.astype(BF16)
    return hi, (x - hi.astype(F32)).astype(BF16)


def kernel(
    rows, cols,
    anc_hbm, panel_hbm, coup_hbm, piv_hbm, lists,
    out_col, out_dia, out_link,
    anc, masked, coup, piv, load_sem,
    held, via, colbuf, blkbuf, col_a, blk_a, col_b, blk_b, z_in, z_mid,
    hi_buf, lo_buf,
    own_up, own_dn, own_rx, via_up, via_dn, via_rx, cross_tx, cross_rx,
    cola_tx, cola_rx, blka_tx, blka_rx, colb_tx, colb_rx, blkb_tx, blkb_rx,
    zi_tx, zo_tx, zin_rx, zmid_rx,
):
    sups, rows_local, width = masked.shape
    half = rows_local // 2
    q = rows // cols
    nx = cols // CORES
    share = rows_local // cols
    band = width // cols
    pieces = 2 * sups - 1
    r = lax.axis_index("row")
    c = lax.axis_index("col")
    x = c // CORES
    k = c % CORES
    mate = x * CORES + (1 - k)
    other = (x + 1 - 2 * (x % 2)) * CORES + k
    mid = rows // 2
    low = r < mid
    inner = jnp.where(low, r + 1, r - 1)
    outer = jnp.where(low, r - 1, r + 1)
    is_mid = jnp.logical_or(r == mid - 1, r == mid)
    has_outer = jnp.logical_and(r > 0, r < rows - 1)

    loads = [
        pltpu.make_async_copy(src, dst, load_sem.at[i])
        for i, (src, dst) in enumerate(
            [(panel_hbm, masked), (anc_hbm, anc), (coup_hbm, coup), (piv_hbm, piv)]
        )
    ]
    for load in loads:
        load.start()

    barrier = pltpu.get_barrier_semaphore()

    def greet(row, col):
        pl.semaphore_signal(barrier, inc=1, device_id={"row": row, "col": col}, device_id_type=MESH)

    @pl.when(r > 0)
    def _():
        greet(r - 1, c)

    @pl.when(r < rows - 1)
    def _():
        greet(r + 1, c)

    greet(r, mate)
    for dx in range(1, nx):
        greet(r, lax.rem(x + dx, nx) * CORES + k)

    tiles = rows_local // width
    names = lists[...]
    member = []
    for t in range(tiles):
        tile = r * tiles + t
        member.append(jnp.max(jnp.where(names == tile, F32(1), F32(0)), axis=1, keepdims=True))
    loads[0].wait()
    for s in range(sups):
        for t in range(tiles):
            sl = pl.ds(t * width, width)
            m = member[t][s:s + 1, :].astype(BF16)
            masked[s, sl, :] = masked[s, sl, :] * m

    for j in range(q):
        @pl.when(c * q + j == r)
        def _():
            for s in range(sups):
                held[j, s, 0] = masked[s, 0:half, :]
                held[j, s, 1] = masked[s, half:, :]

        @pl.when(other * q + j == r)
        def _():
            for s in range(sups):
                via[j, s] = masked[s, half:, :]

    pl.semaphore_wait(
        barrier,
        jnp.where(r > 0, 1, 0) + jnp.where(r < rows - 1, 1, 0) + nx,
    )

    def remote(src, dst, tx, rx, row, col):
        return pltpu.make_async_remote_copy(
            src_ref=src, dst_ref=dst, send_sem=tx, recv_sem=rx,
            device_id={"row": row, "col": col}, device_id_type=MESH,
        )

    def own_copy(j, s, tx, row):
        ref = held.at[j, s, 0]
        return remote(ref, ref, tx.at[j, s], own_rx.at[j, s], row, c)

    def via_copy(j, s, tx, row):
        ref = via.at[j, s]
        return remote(ref, ref, tx.at[j, s], via_rx.at[j, s], row, c)

    def cross_copy(j, s):
        return remote(via.at[j, s], held.at[j, s, 1], cross_tx.at[j, s], cross_rx.at[j, s], r, other)

    def service(s):
        for j in range(q):
            for maker, first, up, dn, crossing in (
                (via_copy, other * q + j, via_up, via_dn, True),
                (own_copy, c * q + j, own_up, own_dn, False),
            ):
                @pl.when(first != r)
                def _():
                    maker(j, s, up, r).wait_recv()

                @pl.when(jnp.logical_and(first <= r, r < rows - 1))
                def _():
                    maker(j, s, up, r + 1).start()

                @pl.when(jnp.logical_and(first >= r, r > 0))
                def _():
                    maker(j, s, dn, r - 1).start()

                if crossing:
                    @pl.when(first != r)
                    def _():
                        cross_copy(j, s).start()

    def col_a_copy(s):
        return remote(colbuf.at[s, 1 - k], col_a.at[s], cola_tx.at[s], cola_rx.at[s], r, mate)

    def blk_a_copy(i):
        return remote(blkbuf.at[i, 1 - k], blk_a.at[i], blka_tx.at[i], blka_rx.at[i], r, mate)

    def col_b_copy(s, dx):
        to = lax.rem(x + dx, nx)
        return remote(colbuf.at[s, k, to], col_b.at[s, dx - 1], colb_tx.at[s, dx - 1],
                      colb_rx.at[s, dx - 1], r, to * CORES + k)

    def blk_b_copy(i, dx):
        to = lax.rem(x + dx, nx)
        return remote(blkbuf.at[i, k, to], blk_b.at[i, dx - 1], blkb_tx.at[i, dx - 1],
                      blkb_rx.at[i, dx - 1], r, to * CORES + k)

    here = jnp.where(jnp.logical_and(r == 0, c == 0), F32(1), F32(0))

    def put_piece(i, value):
        for to in range(cols):
            blkbuf[i, to % CORES, to // CORES] = value[to * band:(to + 1) * band, :]
        blk_a_copy(i).start()

    def compute(s, before):
        for j in range(q):
            @pl.when(c * q + j != r)
            def _():
                cross_copy(j, s).wait_recv()
        if s == 0:
            loads[1].wait()
            loads[2].wait()
            loads[3].wait()
        image = None
        for j in range(q):
            block = held[j, s].reshape(rows_local, width)
            term = dot(anc[:, j * rows_local:(j + 1) * rows_local], block)
            image = term if image is None else image + term
        if s > 0:
            link = coup[s - 1]
            image = image + dot(hi_buf[s - 1], link) + dot(lo_buf[s - 1], link)
        for t in range(tiles):
            sl = slice(t * width, (t + 1) * width)
            value = image[sl, :] * (-member[t][s:s + 1, :])
            hi, lo = split(value)
            hi_buf[s, sl, :] = hi
            lo_buf[s, sl, :] = lo
            per = width // share
            for u in range(per):
                to = t * per + u
                colbuf[s, to % CORES, to // CORES] = value[u * share:(u + 1) * share, :]
        col_a_copy(s).start()
        piece = masked[s]
        gram = dot_t(piece, hi_buf[s]) + dot_t(piece, lo_buf[s])
        base = piv[s].astype(F32) * here - gram
        if s == 0:
            diag = base
        else:
            cross = dot_t(hi_buf[s - 1], piece) + dot_t(lo_buf[s - 1], piece)
            hi, lo = split(before)
            linked = -(cross + dot(hi, link) + dot(lo, link))
            put_piece(2 * s - 1, linked)
            hi, lo = split(linked)
            diag = base - (dot_t(link, hi) + dot_t(link, lo))
        put_piece(2 * s, diag)
        return diag

    def blk_to_x(i):
        blk_a_copy(i).wait_recv()
        blkbuf[i, k] = blkbuf[i, k] + blk_a[i]
        for dx in range(1, nx):
            blk_b_copy(i, dx).start()

    def col_to_x(s):
        col_a_copy(s).wait_recv()
        colbuf[s, k] = colbuf[s, k] + col_a[s]
        for dx in range(1, nx):
            col_b_copy(s, dx).start()

    service(0)
    service(1)
    diag = compute(0, None)
    service(2)
    diag = compute(1, diag)
    blk_to_x(0)
    for s in range(3, sups):
        service(s)
    for s in range(2, sups):
        diag = compute(s, diag)
        blk_to_x(2 * s - 3)
        blk_to_x(2 * s - 2)
    blk_to_x(pieces - 2)
    blk_to_x(pieces - 1)
    for s in range(sups):
        col_to_x(s)

    def to_inner(i, dst, rx):
        return remote(blkbuf.at[i, k, x], dst.at[i], zi_tx.at[i], rx.at[i], inner, c)

    def result(i):
        return out_dia.at[i // 2] if i % 2 == 0 else out_link.at[i // 2]

    def to_outer(i):
        return remote(result(i), z_mid.at[i], zo_tx.at[i], zmid_rx.at[i], outer, c)

    def z_inward(i):
        total = blkbuf[i, k, x]
        for dx in range(1, nx):
            blk_b_copy(i, dx).wait_recv()
            total = total + blk_b[i, dx - 1]
        blkbuf[i, k, x] = total

        @pl.when(has_outer)
        def _():
            to_inner(i, z_in, zin_rx).wait_recv()
            blkbuf[i, k, x] = blkbuf[i, k, x] + z_in[i]

        @pl.when(is_mid)
        def _():
            to_inner(i, z_mid, zmid_rx).start()

        @pl.when(jnp.logical_not(is_mid))
        def _():
            to_inner(i, z_in, zin_rx).start()

    def z_outward(i):
        to_outer(i).wait_recv()

        @pl.when(is_mid)
        def _():
            result(i)[...] = blkbuf[i, k, x] + z_mid[i]

        @pl.when(jnp.logical_not(is_mid))
        def _():
            result(i)[...] = z_mid[i]

        @pl.when(has_outer)
        def _():
            to_outer(i).start()

    lag = 2
    for i in range(pieces + lag):
        if i < pieces:
            z_inward(i)
        if i >= lag:
            z_outward(i - lag)

    for s in range(sups):
        total = colbuf[s, k, x]
        for dx in range(1, nx):
            col_b_copy(s, dx).wait_recv()
            total = total + col_b[s, dx - 1]
        out_col[s] = total

    for s in range(sups):
        for j in range(q):
            for maker, first, up, dn, crossing in (
                (via_copy, other * q + j, via_up, via_dn, True),
                (own_copy, c * q + j, own_up, own_dn, False),
            ):
                @pl.when(jnp.logical_and(first <= r, r < rows - 1))
                def _():
                    maker(j, s, up, r + 1).wait_send()

                @pl.when(jnp.logical_and(first >= r, r > 0))
                def _():
                    maker(j, s, dn, r - 1).wait_send()

                if crossing:
                    @pl.when(first != r)
                    def _():
                        cross_copy(j, s).wait_send()
        col_a_copy(s).wait_send()
        for dx in range(1, nx):
            col_b_copy(s, dx).wait_send()
    for i in range(pieces):
        blk_a_copy(i).wait_send()
        for dx in range(1, nx):
            blk_b_copy(i, dx).wait_send()
        to_inner(i, z_in, zin_rx).wait_send()

        @pl.when(has_outer)
        def _():
            to_outer(i).wait_send()


def shards(rows, cols, ancestors, panel, coupling, pivots, tile_lists):
    sups, rows_local, width = panel.shape
    q = rows // cols
    nx = cols // CORES
    share = rows_local // cols
    band = width // cols
    pieces = 2 * sups - 1
    half = rows_local // 2
    dma = lambda *shape: pltpu.SemaphoreType.DMA(shape)
    hbm = pl.BlockSpec(memory_space=pl.ANY)
    vmem = pl.BlockSpec(memory_space=pltpu.VMEM)
    return pl.pallas_call(
        functools.partial(kernel, rows, cols),
        out_shape=(
            jax.ShapeDtypeStruct((sups, share, width), F32),
            jax.ShapeDtypeStruct((sups, band, width), F32),
            jax.ShapeDtypeStruct((sups - 1, band, width), F32),
        ),
        in_specs=[hbm, hbm, hbm, hbm, vmem],
        out_specs=(vmem, vmem, vmem),
        scratch_shapes=[
            pltpu.VMEM(ancestors.shape, BF16),
            pltpu.VMEM(panel.shape, BF16),
            pltpu.VMEM(coupling.shape, BF16),
            pltpu.VMEM(pivots.shape, BF16),
            dma(4),
            pltpu.VMEM((q, sups, 2, half, width), BF16),
            pltpu.VMEM((q, sups, half, width), BF16),
            pltpu.VMEM((sups, CORES, nx, share, width), F32),
            pltpu.VMEM((pieces, CORES, nx, band, width), F32),
            pltpu.VMEM((sups, nx, share, width), F32),
            pltpu.VMEM((pieces, nx, band, width), F32),
            pltpu.VMEM((sups, nx - 1, share, width), F32),
            pltpu.VMEM((pieces, nx - 1, band, width), F32),
            pltpu.VMEM((pieces, band, width), F32),
            pltpu.VMEM((pieces, band, width), F32),
            pltpu.VMEM((sups, rows_local, width), BF16),
            pltpu.VMEM((sups, rows_local, width), BF16),
            dma(q, sups), dma(q, sups), dma(q, sups),
            dma(q, sups), dma(q, sups), dma(q, sups),
            dma(q, sups), dma(q, sups),
            dma(sups), dma(sups), dma(pieces), dma(pieces),
            dma(sups, nx - 1), dma(sups, nx - 1), dma(pieces, nx - 1), dma(pieces, nx - 1),
            dma(pieces), dma(pieces), dma(pieces), dma(pieces),
        ],
        compiler_params=pltpu.CompilerParams(
            collective_id=0, has_side_effects=True, vmem_limit_bytes=56 * 1024 * 1024
        ),
    )(ancestors, panel, coupling, pivots, tile_lists)


def solution(mesh):
    placed = (
        P(("pole", "row"), "col"),
        P(None, ("pole", "row"), None),
        P("pole", None, None),
        P("pole", None, None),
        P(),
    )
    return jax.shard_map(
        functools.partial(shards, mesh.shape["row"], mesh.shape["col"]),
        mesh=mesh,
        in_specs=placed,
        out_specs=(
            P(None, ("pole", "row", "col"), None),
            P("pole", "col", None),
            P("pole", "col", None),
        ),
        check_vma=False,
    )
```

```python
import functools

import jax
import jax.numpy as jnp
from jax import lax
from jax.experimental import pallas as pl
from jax.experimental.pallas import tpu as pltpu
from jax.sharding import PartitionSpec as P

F32 = jnp.float32
BF16 = jnp.bfloat16
MESH = pl.DeviceIdType.MESH
CORES = 2


def dot(a, b):
    return lax.dot_general(a, b, (((1,), (0,)), ((), ())), preferred_element_type=F32)


def dot_t(a, b):
    return lax.dot_general(a, b, (((0,), (0,)), ((), ())), preferred_element_type=F32)


def split(x):
    hi = x.astype(BF16)
    return hi, (x - hi.astype(F32)).astype(BF16)


def kernel(
    rows, cols,
    anc_hbm, panel_hbm, coup_hbm, piv_hbm, lists,
    out_col, out_dia, out_link,
    anc, masked, coup, piv, load_sem,
    held, colbuf, blkbuf, col_a, blk_a, col_b, blk_b, z_in, z_mid,
    hi_buf, lo_buf,
    own_up, own_dn, own_rx,
    cola_tx, cola_rx, blka_tx, blka_rx, colb_tx, colb_rx, blkb_tx, blkb_rx,
    zi_tx, zo_tx, zin_rx, zmid_rx,
):
    sups, rows_local, width = masked.shape
    half = rows_local // 2
    q = rows // cols
    nx = cols // CORES
    share = rows_local // cols
    band = width // cols
    pieces = 2 * sups - 1
    r = lax.axis_index("row")
    c = lax.axis_index("col")
    x = c // CORES
    k = c % CORES
    mate = x * CORES + (1 - k)
    mid = rows // 2
    low = r < mid
    inner = jnp.where(low, r + 1, r - 1)
    outer = jnp.where(low, r - 1, r + 1)
    is_mid = jnp.logical_or(r == mid - 1, r == mid)
    has_outer = jnp.logical_and(r > 0, r < rows - 1)

    loads = [
        pltpu.make_async_copy(src, dst, load_sem.at[i])
        for i, (src, dst) in enumerate(
            [(panel_hbm, masked), (anc_hbm, anc), (coup_hbm, coup), (piv_hbm, piv)]
        )
    ]
    for load in loads:
        load.start()

    barrier = pltpu.get_barrier_semaphore()

    def greet(row, col):
        pl.semaphore_signal(barrier, inc=1, device_id={"row": row, "col": col}, device_id_type=MESH)

    @pl.when(r > 0)
    def _():
        greet(r - 1, c)

    @pl.when(r < rows - 1)
    def _():
        greet(r + 1, c)

    greet(r, mate)
    for dx in range(1, nx):
        greet(r, lax.rem(x + dx, nx) * CORES + k)

    tiles = rows_local // width
    names = lists[...]
    member = []
    for t in range(tiles):
        tile = r * tiles + t
        member.append(jnp.max(jnp.where(names == tile, F32(1), F32(0)), axis=1, keepdims=True))
    loads[0].wait()
    for s in range(sups):
        for t in range(tiles):
            sl = pl.ds(t * width, width)
            m = member[t][s:s + 1, :].astype(BF16)
            masked[s, sl, :] = masked[s, sl, :] * m

    for j in range(q):
        @pl.when(c * q + j == r)
        def _():
            for s in range(sups):
                held[j, s, 0] = masked[s, 0:half, :]
                held[j, s, 1] = masked[s, half:, :]

    pl.semaphore_wait(
        barrier,
        jnp.where(r > 0, 1, 0) + jnp.where(r < rows - 1, 1, 0) + nx,
    )

    def remote(src, dst, tx, rx, row, col):
        return pltpu.make_async_remote_copy(
            src_ref=src, dst_ref=dst, send_sem=tx, recv_sem=rx,
            device_id={"row": row, "col": col}, device_id_type=MESH,
        )

    def own_copy(j, s, h, tx, row):
        ref = held.at[j, s, h]
        return remote(ref, ref, tx.at[j, s, h], own_rx.at[j, s, h], row, c)

    chunks = [(j, s, h) for s in range(sups) for j in range(q) for h in range(2)]

    for j, s, h in chunks:
        @pl.when(jnp.logical_and(c * q + j == r, r < rows - 1))
        def _():
            own_copy(j, s, h, own_up, r + 1).start()

        @pl.when(jnp.logical_and(c * q + j == r, r > 0))
        def _():
            own_copy(j, s, h, own_dn, r - 1).start()

    def relay(sup):
        for j, s, h in chunks:
            if s != sup:
                continue
            first = c * q + j

            @pl.when(first != r)
            def _():
                own_copy(j, s, h, own_up, r).wait_recv()

            @pl.when(jnp.logical_and(first < r, r < rows - 1))
            def _():
                own_copy(j, s, h, own_up, r + 1).start()

            @pl.when(jnp.logical_and(first > r, r > 0))
            def _():
                own_copy(j, s, h, own_dn, r - 1).start()

    def col_a_copy(s):
        return remote(colbuf.at[s, 1 - k], col_a.at[s], cola_tx.at[s], cola_rx.at[s], r, mate)

    def blk_a_copy(i):
        return remote(blkbuf.at[i, 1 - k], blk_a.at[i], blka_tx.at[i], blka_rx.at[i], r, mate)

    def col_b_copy(s, dx):
        to = lax.rem(x + dx, nx)
        return remote(colbuf.at[s, k, to], col_b.at[s, dx - 1], colb_tx.at[s, dx - 1],
                      colb_rx.at[s, dx - 1], r, to * CORES + k)

    def blk_b_copy(i, dx):
        to = lax.rem(x + dx, nx)
        return remote(blkbuf.at[i, k, to], blk_b.at[i, dx - 1], blkb_tx.at[i, dx - 1],
                      blkb_rx.at[i, dx - 1], r, to * CORES + k)

    here = jnp.where(jnp.logical_and(r == 0, c == 0), F32(1), F32(0))

    def put_piece(i, value):
        for to in range(cols):
            blkbuf[i, to % CORES, to // CORES] = value[to * band:(to + 1) * band, :]
        blk_a_copy(i).start()

    def compute(s, before):
        if s == 0:
            loads[1].wait()
            loads[2].wait()
            loads[3].wait()
        image = None
        for j in range(q):
            block = held[j, s].reshape(rows_local, width)
            term = dot(anc[:, j * rows_local:(j + 1) * rows_local], block)
            image = term if image is None else image + term
        if s > 0:
            link = coup[s - 1]
            image = image + dot(hi_buf[s - 1], link) + dot(lo_buf[s - 1], link)
        for t in range(tiles):
            sl = slice(t * width, (t + 1) * width)
            value = image[sl, :] * (-member[t][s:s + 1, :])
            hi, lo = split(value)
            hi_buf[s, sl, :] = hi
            lo_buf[s, sl, :] = lo
            per = width // share
            for u in range(per):
                to = t * per + u
                colbuf[s, to % CORES, to // CORES] = value[u * share:(u + 1) * share, :]
        col_a_copy(s).start()
        piece = masked[s]
        gram = dot_t(piece, hi_buf[s]) + dot_t(piece, lo_buf[s])
        base = piv[s].astype(F32) * here - gram
        if s == 0:
            diag = base
        else:
            cross = dot_t(hi_buf[s - 1], piece) + dot_t(lo_buf[s - 1], piece)
            hi, lo = split(before)
            linked = -(cross + dot(hi, link) + dot(lo, link))
            put_piece(2 * s - 1, linked)
            hi, lo = split(linked)
            diag = base - (dot_t(link, hi) + dot_t(link, lo))
        put_piece(2 * s, diag)
        return diag

    def blk_to_x(i):
        blk_a_copy(i).wait_recv()
        blkbuf[i, k] = blkbuf[i, k] + blk_a[i]
        for dx in range(1, nx):
            blk_b_copy(i, dx).start()

    def col_to_x(s):
        col_a_copy(s).wait_recv()
        colbuf[s, k] = colbuf[s, k] + col_a[s]
        for dx in range(1, nx):
            col_b_copy(s, dx).start()

    def to_inner(i, dst, rx):
        return remote(blkbuf.at[i, k, x], dst.at[i], zi_tx.at[i], rx.at[i], inner, c)

    def result(i):
        return out_dia.at[i // 2] if i % 2 == 0 else out_link.at[i // 2]

    def to_outer(i):
        return remote(result(i), z_mid.at[i], zo_tx.at[i], zmid_rx.at[i], outer, c)

    def z_inward(i):
        total = blkbuf[i, k, x]
        for dx in range(1, nx):
            blk_b_copy(i, dx).wait_recv()
            total = total + blk_b[i, dx - 1]
        blkbuf[i, k, x] = total

        @pl.when(has_outer)
        def _():
            to_inner(i, z_in, zin_rx).wait_recv()
            blkbuf[i, k, x] = blkbuf[i, k, x] + z_in[i]

        @pl.when(is_mid)
        def _():
            to_inner(i, z_mid, zmid_rx).start()

        @pl.when(jnp.logical_not(is_mid))
        def _():
            to_inner(i, z_in, zin_rx).start()

    def z_outward(i):
        to_outer(i).wait_recv()

        @pl.when(is_mid)
        def _():
            result(i)[...] = blkbuf[i, k, x] + z_mid[i]

        @pl.when(jnp.logical_not(is_mid))
        def _():
            result(i)[...] = z_mid[i]

        @pl.when(has_outer)
        def _():
            to_outer(i).start()

    def names_of(s):
        return [0] if s == 0 else [2 * s - 1, 2 * s]

    diag = None
    for s in range(sups):
        relay(s)
        diag = compute(s, diag)
        if s >= 2:
            for i in names_of(s - 2):
                z_inward(i)
        if s >= 1:
            for i in names_of(s - 1):
                blk_to_x(i)
            col_to_x(s - 1)
        if s >= 3:
            for i in names_of(s - 3):
                z_outward(i)
    for i in names_of(sups - 1):
        blk_to_x(i)
    for s in (sups - 2, sups - 1):
        for i in names_of(s):
            z_inward(i)
        if s == sups - 2:
            col_to_x(sups - 1)
    for s in range(max(sups - 3, 0), sups):
        for i in names_of(s):
            z_outward(i)

    for s in range(sups):
        total = colbuf[s, k, x]
        for dx in range(1, nx):
            col_b_copy(s, dx).wait_recv()
            total = total + col_b[s, dx - 1]
        out_col[s] = total

    for s in range(sups):
        col_a_copy(s).wait_send()
        for dx in range(1, nx):
            col_b_copy(s, dx).wait_send()
    for j, s, h in chunks:
        @pl.when(jnp.logical_and(c * q + j <= r, r < rows - 1))
        def _():
            own_copy(j, s, h, own_up, r + 1).wait_send()

        @pl.when(jnp.logical_and(c * q + j >= r, r > 0))
        def _():
            own_copy(j, s, h, own_dn, r - 1).wait_send()

    for i in range(pieces):
        blk_a_copy(i).wait_send()
        for dx in range(1, nx):
            blk_b_copy(i, dx).wait_send()
        to_inner(i, z_in, zin_rx).wait_send()

        @pl.when(has_outer)
        def _():
            to_outer(i).wait_send()


def shards(rows, cols, ancestors, panel, coupling, pivots, tile_lists):
    sups, rows_local, width = panel.shape
    q = rows // cols
    nx = cols // CORES
    share = rows_local // cols
    band = width // cols
    pieces = 2 * sups - 1
    half = rows_local // 2
    dma = lambda *shape: pltpu.SemaphoreType.DMA(shape)
    hbm = pl.BlockSpec(memory_space=pl.ANY)
    vmem = pl.BlockSpec(memory_space=pltpu.VMEM)
    return pl.pallas_call(
        functools.partial(kernel, rows, cols),
        out_shape=(
            jax.ShapeDtypeStruct((sups, share, width), F32),
            jax.ShapeDtypeStruct((sups, band, width), F32),
            jax.ShapeDtypeStruct((sups - 1, band, width), F32),
        ),
        in_specs=[hbm, hbm, hbm, hbm, vmem],
        out_specs=(vmem, vmem, vmem),
        scratch_shapes=[
            pltpu.VMEM(ancestors.shape, BF16),
            pltpu.VMEM(panel.shape, BF16),
            pltpu.VMEM(coupling.shape, BF16),
            pltpu.VMEM(pivots.shape, BF16),
            dma(4),
            pltpu.VMEM((q, sups, 2, half, width), BF16),
            pltpu.VMEM((sups, CORES, nx, share, width), F32),
            pltpu.VMEM((pieces, CORES, nx, band, width), F32),
            pltpu.VMEM((sups, nx, share, width), F32),
            pltpu.VMEM((pieces, nx, band, width), F32),
            pltpu.VMEM((sups, nx - 1, share, width), F32),
            pltpu.VMEM((pieces, nx - 1, band, width), F32),
            pltpu.VMEM((pieces, band, width), F32),
            pltpu.VMEM((pieces, band, width), F32),
            pltpu.VMEM((sups, rows_local, width), BF16),
            pltpu.VMEM((sups, rows_local, width), BF16),
            dma(q, sups, 2), dma(q, sups, 2), dma(q, sups, 2),
            dma(sups), dma(sups), dma(pieces), dma(pieces),
            dma(sups, nx - 1), dma(sups, nx - 1), dma(pieces, nx - 1), dma(pieces, nx - 1),
            dma(pieces), dma(pieces), dma(pieces), dma(pieces),
        ],
        compiler_params=pltpu.CompilerParams(
            collective_id=0, has_side_effects=True, vmem_limit_bytes=56 * 1024 * 1024
        ),
    )(ancestors, panel, coupling, pivots, tile_lists)


def solution(mesh):
    placed = (
        P(("pole", "row"), "col"),
        P(None, ("pole", "row"), None),
        P("pole", None, None),
        P("pole", None, None),
        P(),
    )
    return jax.shard_map(
        functools.partial(shards, mesh.shape["row"], mesh.shape["col"]),
        mesh=mesh,
        in_specs=placed,
        out_specs=(
            P(None, ("pole", "row", "col"), None),
            P("pole", "col", None),
            P("pole", "col", None),
        ),
        check_vma=False,
    )
```

```python
import functools

import jax
import jax.numpy as jnp
from jax import lax
from jax.experimental import pallas as pl
from jax.experimental.pallas import tpu as pltpu
from jax.sharding import PartitionSpec as P

F32 = jnp.float32
BF16 = jnp.bfloat16
MESH = pl.DeviceIdType.MESH
CORES = 2


def dot(a, b):
    return lax.dot_general(a, b, (((1,), (0,)), ((), ())), preferred_element_type=F32)


def dot_t(a, b):
    return lax.dot_general(a, b, (((0,), (0,)), ((), ())), preferred_element_type=F32)


def split(x):
    hi = x.astype(BF16)
    return hi, (x - hi.astype(F32)).astype(BF16)


def kernel(
    rows, cols,
    anc_hbm, panel_hbm, coup_hbm, piv_hbm, lists,
    out_col, out_dia, out_link,
    anc, masked, coup, piv, load_sem,
    held, colbuf, blkbuf, col_a, blk_a, col_b, blk_b, z_in, z_mid,
    hi_buf, lo_buf,
    own_up, own_dn, own_rx,
    cola_tx, cola_rx, blka_tx, blka_rx, colb_tx, colb_rx, blkb_tx, blkb_rx,
    zi_tx, zo_tx, zin_rx, zmid_rx,
):
    sups, rows_local, width = masked.shape
    half = rows_local // 2
    q = rows // cols
    nx = cols // CORES
    share = rows_local // cols
    band = width // cols
    pieces = 2 * sups - 1
    r = lax.axis_index("row")
    c = lax.axis_index("col")
    x = c // CORES
    k = c % CORES
    mate = x * CORES + (1 - k)
    mid = rows // 2
    low = r < mid
    inner = jnp.where(low, r + 1, r - 1)
    outer = jnp.where(low, r - 1, r + 1)
    is_mid = jnp.logical_or(r == mid - 1, r == mid)
    has_outer = jnp.logical_and(r > 0, r < rows - 1)

    loads = [
        pltpu.make_async_copy(src, dst, load_sem.at[i])
        for i, (src, dst) in enumerate(
            [(panel_hbm.at[s], masked.at[s]) for s in range(sups)]
            + [(anc_hbm, anc), (coup_hbm, coup), (piv_hbm, piv)]
        )
    ]
    for load in loads:
        load.start()

    barrier = pltpu.get_barrier_semaphore()

    def greet(row, col):
        pl.semaphore_signal(barrier, inc=1, device_id={"row": row, "col": col}, device_id_type=MESH)

    @pl.when(r > 0)
    def _():
        greet(r - 1, c)

    @pl.when(r < rows - 1)
    def _():
        greet(r + 1, c)

    greet(r, mate)
    for dx in range(1, nx):
        greet(r, lax.rem(x + dx, nx) * CORES + k)

    tiles = rows_local // width
    names = lists[...]
    member = []
    for t in range(tiles):
        tile = r * tiles + t
        member.append(jnp.max(jnp.where(names == tile, F32(1), F32(0)), axis=1, keepdims=True))
    pl.semaphore_wait(
        barrier,
        jnp.where(r > 0, 1, 0) + jnp.where(r < rows - 1, 1, 0) + nx,
    )

    def remote(src, dst, tx, rx, row, col):
        return pltpu.make_async_remote_copy(
            src_ref=src, dst_ref=dst, send_sem=tx, recv_sem=rx,
            device_id={"row": row, "col": col}, device_id_type=MESH,
        )

    def own_copy(j, s, h, tx, row):
        ref = held.at[j, s, h]
        return remote(ref, ref, tx.at[j, s, h], own_rx.at[j, s, h], row, c)

    chunks = [(j, s, h) for s in range(sups) for j in range(q) for h in range(2)]

    for s in range(sups):
        loads[s].wait()
        for t in range(tiles):
            sl = pl.ds(t * width, width)
            m = member[t][s:s + 1, :].astype(BF16)
            masked[s, sl, :] = masked[s, sl, :] * m
        for j in range(q):
            @pl.when(c * q + j == r)
            def _():
                held[j, s, 0] = masked[s, 0:half, :]
                held[j, s, 1] = masked[s, half:, :]

                for h in range(2):
                    @pl.when(r < rows - 1)
                    def _():
                        own_copy(j, s, h, own_up, r + 1).start()

                    @pl.when(r > 0)
                    def _():
                        own_copy(j, s, h, own_dn, r - 1).start()

    def relay(sup):
        for j, s, h in chunks:
            if s != sup:
                continue
            first = c * q + j

            @pl.when(first != r)
            def _():
                own_copy(j, s, h, own_up, r).wait_recv()

            @pl.when(jnp.logical_and(first < r, r < rows - 1))
            def _():
                own_copy(j, s, h, own_up, r + 1).start()

            @pl.when(jnp.logical_and(first > r, r > 0))
            def _():
                own_copy(j, s, h, own_dn, r - 1).start()

    def col_a_copy(s):
        return remote(colbuf.at[s, 1 - k], col_a.at[s], cola_tx.at[s], cola_rx.at[s], r, mate)

    def blk_a_copy(i):
        return remote(blkbuf.at[i, 1 - k], blk_a.at[i], blka_tx.at[i], blka_rx.at[i], r, mate)

    def col_b_copy(s, dx):
        to = lax.rem(x + dx, nx)
        return remote(colbuf.at[s, k, to], col_b.at[s, dx - 1], colb_tx.at[s, dx - 1],
                      colb_rx.at[s, dx - 1], r, to * CORES + k)

    def blk_b_copy(i, dx):
        to = lax.rem(x + dx, nx)
        return remote(blkbuf.at[i, k, to], blk_b.at[i, dx - 1], blkb_tx.at[i, dx - 1],
                      blkb_rx.at[i, dx - 1], r, to * CORES + k)

    here = jnp.where(jnp.logical_and(r == 0, c == 0), F32(1), F32(0))

    def put_piece(i, value):
        for to in range(cols):
            blkbuf[i, to % CORES, to // CORES] = value[to * band:(to + 1) * band, :]
        blk_a_copy(i).start()

    def compute(s, before):
        if s == 0:
            for load in loads[sups:]:
                load.wait()
        image = None
        for j in range(q):
            block = held[j, s].reshape(rows_local, width)
            term = dot(anc[:, j * rows_local:(j + 1) * rows_local], block)
            image = term if image is None else image + term
        if s > 0:
            link = coup[s - 1]
            image = image + dot(hi_buf[s - 1], link) + dot(lo_buf[s - 1], link)
        for t in range(tiles):
            sl = slice(t * width, (t + 1) * width)
            value = image[sl, :] * (-member[t][s:s + 1, :])
            hi, lo = split(value)
            hi_buf[s, sl, :] = hi
            lo_buf[s, sl, :] = lo
            per = width // share
            for u in range(per):
                to = t * per + u
                colbuf[s, to % CORES, to // CORES] = value[u * share:(u + 1) * share, :]
        col_a_copy(s).start()
        piece = masked[s]
        gram = dot_t(piece, hi_buf[s]) + dot_t(piece, lo_buf[s])
        base = piv[s].astype(F32) * here - gram
        if s == 0:
            diag = base
        else:
            cross = dot_t(hi_buf[s - 1], piece) + dot_t(lo_buf[s - 1], piece)
            hi, lo = split(before)
            linked = -(cross + dot(hi, link) + dot(lo, link))
            put_piece(2 * s - 1, linked)
            hi, lo = split(linked)
            diag = base - (dot_t(link, hi) + dot_t(link, lo))
        put_piece(2 * s, diag)
        return diag

    def blk_to_x(i):
        blk_a_copy(i).wait_recv()
        blkbuf[i, k] = blkbuf[i, k] + blk_a[i]
        for dx in range(1, nx):
            blk_b_copy(i, dx).start()

    def col_to_x(s):
        col_a_copy(s).wait_recv()
        colbuf[s, k] = colbuf[s, k] + col_a[s]
        for dx in range(1, nx):
            col_b_copy(s, dx).start()

    def to_inner(i, dst, rx):
        return remote(blkbuf.at[i, k, x], dst.at[i], zi_tx.at[i], rx.at[i], inner, c)

    def result(i):
        return out_dia.at[i // 2] if i % 2 == 0 else out_link.at[i // 2]

    def to_outer(i):
        return remote(result(i), z_mid.at[i], zo_tx.at[i], zmid_rx.at[i], outer, c)

    def z_inward(i):
        total = blkbuf[i, k, x]
        for dx in range(1, nx):
            blk_b_copy(i, dx).wait_recv()
            total = total + blk_b[i, dx - 1]
        blkbuf[i, k, x] = total

        @pl.when(has_outer)
        def _():
            to_inner(i, z_in, zin_rx).wait_recv()
            blkbuf[i, k, x] = blkbuf[i, k, x] + z_in[i]

        @pl.when(is_mid)
        def _():
            to_inner(i, z_mid, zmid_rx).start()

        @pl.when(jnp.logical_not(is_mid))
        def _():
            to_inner(i, z_in, zin_rx).start()

    def z_outward(i):
        to_outer(i).wait_recv()

        @pl.when(is_mid)
        def _():
            result(i)[...] = blkbuf[i, k, x] + z_mid[i]

        @pl.when(jnp.logical_not(is_mid))
        def _():
            result(i)[...] = z_mid[i]

        @pl.when(has_outer)
        def _():
            to_outer(i).start()

    def names_of(s):
        return [0] if s == 0 else [2 * s - 1, 2 * s]

    diag = None
    relay(0)
    for s in range(sups):
        diag = compute(s, diag)
        if s + 1 < sups:
            relay(s + 1)
        for i in names_of(s):
            blk_to_x(i)
        if s >= 2:
            for i in names_of(s - 2):
                z_inward(i)
        if s < sups - 1:
            col_to_x(s)

    def finish(s):
        total = colbuf[s, k, x]
        for dx in range(1, nx):
            col_b_copy(s, dx).wait_recv()
            total = total + col_b[s, dx - 1]
        out_col[s] = total

    col_to_x(sups - 1)
    begun = pieces - 4

    @pl.when(has_outer)
    def _():
        behind = 0
        for i in range(begun, pieces):
            z_inward(i)
            while behind < i - 1:
                z_outward(behind)
                behind += 1
        for i in range(behind, pieces):
            z_outward(i)

    @pl.when(jnp.logical_not(has_outer))
    def _():
        for i in range(begun, pieces):
            z_inward(i)
        for i in range(pieces):
            z_outward(i)

    for s in range(sups):
        finish(s)

    for s in range(sups):
        col_a_copy(s).wait_send()
        for dx in range(1, nx):
            col_b_copy(s, dx).wait_send()
    for j, s, h in chunks:
        @pl.when(jnp.logical_and(c * q + j <= r, r < rows - 1))
        def _():
            own_copy(j, s, h, own_up, r + 1).wait_send()

        @pl.when(jnp.logical_and(c * q + j >= r, r > 0))
        def _():
            own_copy(j, s, h, own_dn, r - 1).wait_send()

    for i in range(pieces):
        blk_a_copy(i).wait_send()
        for dx in range(1, nx):
            blk_b_copy(i, dx).wait_send()
        to_inner(i, z_in, zin_rx).wait_send()

        @pl.when(has_outer)
        def _():
            to_outer(i).wait_send()


def shards(rows, cols, ancestors, panel, coupling, pivots, tile_lists):
    sups, rows_local, width = panel.shape
    q = rows // cols
    nx = cols // CORES
    share = rows_local // cols
    band = width // cols
    pieces = 2 * sups - 1
    half = rows_local // 2
    dma = lambda *shape: pltpu.SemaphoreType.DMA(shape)
    hbm = pl.BlockSpec(memory_space=pl.ANY)
    vmem = pl.BlockSpec(memory_space=pltpu.VMEM)
    return pl.pallas_call(
        functools.partial(kernel, rows, cols),
        out_shape=(
            jax.ShapeDtypeStruct((sups, share, width), F32),
            jax.ShapeDtypeStruct((sups, band, width), F32),
            jax.ShapeDtypeStruct((sups - 1, band, width), F32),
        ),
        in_specs=[hbm, hbm, hbm, hbm, vmem],
        out_specs=(vmem, vmem, vmem),
        scratch_shapes=[
            pltpu.VMEM(ancestors.shape, BF16),
            pltpu.VMEM(panel.shape, BF16),
            pltpu.VMEM(coupling.shape, BF16),
            pltpu.VMEM(pivots.shape, BF16),
            dma(sups + 3),
            pltpu.VMEM((q, sups, 2, half, width), BF16),
            pltpu.VMEM((sups, CORES, nx, share, width), F32),
            pltpu.VMEM((pieces, CORES, nx, band, width), F32),
            pltpu.VMEM((sups, nx, share, width), F32),
            pltpu.VMEM((pieces, nx, band, width), F32),
            pltpu.VMEM((sups, nx - 1, share, width), F32),
            pltpu.VMEM((pieces, nx - 1, band, width), F32),
            pltpu.VMEM((pieces, band, width), F32),
            pltpu.VMEM((pieces, band, width), F32),
            pltpu.VMEM((sups, rows_local, width), BF16),
            pltpu.VMEM((sups, rows_local, width), BF16),
            dma(q, sups, 2), dma(q, sups, 2), dma(q, sups, 2),
            dma(sups), dma(sups), dma(pieces), dma(pieces),
            dma(sups, nx - 1), dma(sups, nx - 1), dma(pieces, nx - 1), dma(pieces, nx - 1),
            dma(pieces), dma(pieces), dma(pieces), dma(pieces),
        ],
        compiler_params=pltpu.CompilerParams(
            collective_id=0, has_side_effects=True, vmem_limit_bytes=56 * 1024 * 1024
        ),
    )(ancestors, panel, coupling, pivots, tile_lists)


def solution(mesh):
    placed = (
        P(("pole", "row"), "col"),
        P(None, ("pole", "row"), None),
        P("pole", None, None),
        P("pole", None, None),
        P(),
    )
    return jax.shard_map(
        functools.partial(shards, mesh.shape["row"], mesh.shape["col"]),
        mesh=mesh,
        in_specs=placed,
        out_specs=(
            P(None, ("pole", "row", "col"), None),
            P("pole", "col", None),
            P("pole", "col", None),
        ),
        check_vma=False,
    )
```

```python
import functools

import jax
import jax.numpy as jnp
from jax import lax
from jax.experimental import pallas as pl
from jax.experimental.pallas import tpu as pltpu
from jax.sharding import PartitionSpec as P

F32 = jnp.float32
BF16 = jnp.bfloat16
MESH = pl.DeviceIdType.MESH
CORES = 2
PARTS = 4


def dot(a, b):
    return lax.dot_general(a, b, (((1,), (0,)), ((), ())), preferred_element_type=F32)


def dot_t(a, b):
    return lax.dot_general(a, b, (((0,), (0,)), ((), ())), preferred_element_type=F32)


def split(x):
    hi = x.astype(BF16)
    return hi, (x - hi.astype(F32)).astype(BF16)


def kernel(
    rows, cols,
    anc_hbm, panel_hbm, coup_hbm, piv_hbm, lists,
    out_col, out_dia, out_link,
    anc, masked, coup, piv, load_sem,
    held, colbuf, blkbuf, col_a, blk_a, col_b, blk_b, z_in, z_mid,
    hi_buf, lo_buf,
    own_up, own_dn, own_rx,
    cola_tx, cola_rx, blka_tx, blka_rx, colb_tx, colb_rx, blkb_tx, blkb_rx,
    zi_tx, zo_tx, zin_rx, zmid_rx,
):
    sups, rows_local, width = masked.shape
    half = rows_local // PARTS
    q = rows // cols
    nx = cols // CORES
    share = rows_local // cols
    band = width // cols
    pieces = 2 * sups - 1
    r = lax.axis_index("row")
    c = lax.axis_index("col")
    x = c // CORES
    k = c % CORES
    mate = x * CORES + (1 - k)
    mid = rows // 2
    low = r < mid
    inner = jnp.where(low, r + 1, r - 1)
    outer = jnp.where(low, r - 1, r + 1)
    is_mid = jnp.logical_or(r == mid - 1, r == mid)
    has_outer = jnp.logical_and(r > 0, r < rows - 1)

    loads = [
        pltpu.make_async_copy(src, dst, load_sem.at[i])
        for i, (src, dst) in enumerate(
            [(panel_hbm.at[s], masked.at[s]) for s in range(sups)]
            + [(anc_hbm, anc), (coup_hbm, coup), (piv_hbm, piv)]
        )
    ]
    for load in loads:
        load.start()

    barrier = pltpu.get_barrier_semaphore()

    def greet(row, col):
        pl.semaphore_signal(barrier, inc=1, device_id={"row": row, "col": col}, device_id_type=MESH)

    @pl.when(r > 0)
    def _():
        greet(r - 1, c)

    @pl.when(r < rows - 1)
    def _():
        greet(r + 1, c)

    greet(r, mate)
    for dx in range(1, nx):
        greet(r, lax.rem(x + dx, nx) * CORES + k)

    tiles = rows_local // width
    names = lists[...]
    member = []
    for t in range(tiles):
        tile = r * tiles + t
        member.append(jnp.max(jnp.where(names == tile, F32(1), F32(0)), axis=1, keepdims=True))
    pl.semaphore_wait(
        barrier,
        jnp.where(r > 0, 1, 0) + jnp.where(r < rows - 1, 1, 0) + nx,
    )

    def remote(src, dst, tx, rx, row, col):
        return pltpu.make_async_remote_copy(
            src_ref=src, dst_ref=dst, send_sem=tx, recv_sem=rx,
            device_id={"row": row, "col": col}, device_id_type=MESH,
        )

    def own_copy(j, s, h, tx, row):
        ref = held.at[j, s, h]
        return remote(ref, ref, tx.at[j, s, h], own_rx.at[j, s, h], row, c)

    chunks = [(j, s, h) for s in range(sups) for j in range(q) for h in range(PARTS)]

    for s in range(sups):
        loads[s].wait()
        for t in range(tiles):
            sl = pl.ds(t * width, width)
            m = member[t][s:s + 1, :].astype(BF16)
            masked[s, sl, :] = masked[s, sl, :] * m
        for j in range(q):
            @pl.when(c * q + j == r)
            def _():
                for h in range(PARTS):
                    held[j, s, h] = masked[s, h * half:(h + 1) * half, :]

                for h in range(PARTS):
                    @pl.when(r < rows - 1)
                    def _():
                        own_copy(j, s, h, own_up, r + 1).start()

                    @pl.when(r > 0)
                    def _():
                        own_copy(j, s, h, own_dn, r - 1).start()

    def relay(sup):
        for j, s, h in chunks:
            if s != sup:
                continue
            first = c * q + j

            @pl.when(first != r)
            def _():
                own_copy(j, s, h, own_up, r).wait_recv()

            @pl.when(jnp.logical_and(first < r, r < rows - 1))
            def _():
                own_copy(j, s, h, own_up, r + 1).start()

            @pl.when(jnp.logical_and(first > r, r > 0))
            def _():
                own_copy(j, s, h, own_dn, r - 1).start()

    def col_a_copy(s):
        return remote(colbuf.at[s, 1 - k], col_a.at[s], cola_tx.at[s], cola_rx.at[s], r, mate)

    def blk_a_copy(i):
        return remote(blkbuf.at[i, 1 - k], blk_a.at[i], blka_tx.at[i], blka_rx.at[i], r, mate)

    def col_b_copy(s, dx):
        to = lax.rem(x + dx, nx)
        return remote(colbuf.at[s, k, to], col_b.at[s, dx - 1], colb_tx.at[s, dx - 1],
                      colb_rx.at[s, dx - 1], r, to * CORES + k)

    def blk_b_copy(i, dx):
        to = lax.rem(x + dx, nx)
        return remote(blkbuf.at[i, k, to], blk_b.at[i, dx - 1], blkb_tx.at[i, dx - 1],
                      blkb_rx.at[i, dx - 1], r, to * CORES + k)

    here = jnp.where(jnp.logical_and(r == 0, c == 0), F32(1), F32(0))

    def put_piece(i, value):
        for to in range(cols):
            blkbuf[i, to % CORES, to // CORES] = value[to * band:(to + 1) * band, :]
        blk_a_copy(i).start()

    def compute(s, before):
        if s == 0:
            for load in loads[sups:]:
                load.wait()
        image = None
        for j in range(q):
            block = held[j, s].reshape(rows_local, width)
            term = dot(anc[:, j * rows_local:(j + 1) * rows_local], block)
            image = term if image is None else image + term
        if s > 0:
            link = coup[s - 1]
            image = image + dot(hi_buf[s - 1], link) + dot(lo_buf[s - 1], link)
        for t in range(tiles):
            sl = slice(t * width, (t + 1) * width)
            value = image[sl, :] * (-member[t][s:s + 1, :])
            hi, lo = split(value)
            hi_buf[s, sl, :] = hi
            lo_buf[s, sl, :] = lo
            per = width // share
            for u in range(per):
                to = t * per + u
                colbuf[s, to % CORES, to // CORES] = value[u * share:(u + 1) * share, :]
        col_a_copy(s).start()
        piece = masked[s]
        gram = dot_t(piece, hi_buf[s]) + dot_t(piece, lo_buf[s])
        base = piv[s].astype(F32) * here - gram
        if s == 0:
            diag = base
        else:
            cross = dot_t(hi_buf[s - 1], piece) + dot_t(lo_buf[s - 1], piece)
            hi, lo = split(before)
            linked = -(cross + dot(hi, link) + dot(lo, link))
            put_piece(2 * s - 1, linked)
            hi, lo = split(linked)
            diag = base - (dot_t(link, hi) + dot_t(link, lo))
        put_piece(2 * s, diag)
        return diag

    def blk_to_x(i):
        blk_a_copy(i).wait_recv()
        blkbuf[i, k] = blkbuf[i, k] + blk_a[i]
        for dx in range(1, nx):
            blk_b_copy(i, dx).start()

    def col_to_x(s):
        col_a_copy(s).wait_recv()
        colbuf[s, k] = colbuf[s, k] + col_a[s]
        for dx in range(1, nx):
            col_b_copy(s, dx).start()

    def to_inner(i, dst, rx):
        return remote(blkbuf.at[i, k, x], dst.at[i], zi_tx.at[i], rx.at[i], inner, c)

    def result(i):
        return out_dia.at[i // 2] if i % 2 == 0 else out_link.at[i // 2]

    def to_outer(i):
        return remote(result(i), z_mid.at[i], zo_tx.at[i], zmid_rx.at[i], outer, c)

    def z_inward(i):
        total = blkbuf[i, k, x]
        for dx in range(1, nx):
            blk_b_copy(i, dx).wait_recv()
            total = total + blk_b[i, dx - 1]
        blkbuf[i, k, x] = total

        @pl.when(has_outer)
        def _():
            to_inner(i, z_in, zin_rx).wait_recv()
            blkbuf[i, k, x] = blkbuf[i, k, x] + z_in[i]

        @pl.when(is_mid)
        def _():
            to_inner(i, z_mid, zmid_rx).start()

        @pl.when(jnp.logical_not(is_mid))
        def _():
            to_inner(i, z_in, zin_rx).start()

    def z_outward(i):
        to_outer(i).wait_recv()

        @pl.when(is_mid)
        def _():
            result(i)[...] = blkbuf[i, k, x] + z_mid[i]

        @pl.when(jnp.logical_not(is_mid))
        def _():
            result(i)[...] = z_mid[i]

        @pl.when(has_outer)
        def _():
            to_outer(i).start()

    def names_of(s):
        return [0] if s == 0 else [2 * s - 1, 2 * s]

    diag = None
    relay(0)
    for s in range(sups):
        diag = compute(s, diag)
        if s + 1 < sups:
            relay(s + 1)
        for i in names_of(s):
            blk_to_x(i)
        if s >= 2:
            for i in names_of(s - 2):
                z_inward(i)
        if s < sups - 1:
            col_to_x(s)

    def finish(s):
        total = colbuf[s, k, x]
        for dx in range(1, nx):
            col_b_copy(s, dx).wait_recv()
            total = total + col_b[s, dx - 1]
        out_col[s] = total

    col_to_x(sups - 1)
    begun = pieces - 4

    @pl.when(has_outer)
    def _():
        behind = 0
        for i in range(begun, pieces):
            z_inward(i)
            while behind < i - 1:
                z_outward(behind)
                behind += 1
        for i in range(behind, pieces):
            z_outward(i)

    @pl.when(jnp.logical_not(has_outer))
    def _():
        for i in range(begun, pieces):
            z_inward(i)
        for i in range(pieces):
            z_outward(i)

    for s in range(sups):
        finish(s)

    for s in range(sups):
        col_a_copy(s).wait_send()
        for dx in range(1, nx):
            col_b_copy(s, dx).wait_send()
    for j, s, h in chunks:
        @pl.when(jnp.logical_and(c * q + j <= r, r < rows - 1))
        def _():
            own_copy(j, s, h, own_up, r + 1).wait_send()

        @pl.when(jnp.logical_and(c * q + j >= r, r > 0))
        def _():
            own_copy(j, s, h, own_dn, r - 1).wait_send()

    for i in range(pieces):
        blk_a_copy(i).wait_send()
        for dx in range(1, nx):
            blk_b_copy(i, dx).wait_send()
        to_inner(i, z_in, zin_rx).wait_send()

        @pl.when(has_outer)
        def _():
            to_outer(i).wait_send()


def shards(rows, cols, ancestors, panel, coupling, pivots, tile_lists):
    sups, rows_local, width = panel.shape
    q = rows // cols
    nx = cols // CORES
    share = rows_local // cols
    band = width // cols
    pieces = 2 * sups - 1
    half = rows_local // PARTS
    dma = lambda *shape: pltpu.SemaphoreType.DMA(shape)
    hbm = pl.BlockSpec(memory_space=pl.ANY)
    vmem = pl.BlockSpec(memory_space=pltpu.VMEM)
    return pl.pallas_call(
        functools.partial(kernel, rows, cols),
        out_shape=(
            jax.ShapeDtypeStruct((sups, share, width), F32),
            jax.ShapeDtypeStruct((sups, band, width), F32),
            jax.ShapeDtypeStruct((sups - 1, band, width), F32),
        ),
        in_specs=[hbm, hbm, hbm, hbm, vmem],
        out_specs=(vmem, vmem, vmem),
        scratch_shapes=[
            pltpu.VMEM(ancestors.shape, BF16),
            pltpu.VMEM(panel.shape, BF16),
            pltpu.VMEM(coupling.shape, BF16),
            pltpu.VMEM(pivots.shape, BF16),
            dma(sups + 3),
            pltpu.VMEM((q, sups, PARTS, half, width), BF16),
            pltpu.VMEM((sups, CORES, nx, share, width), F32),
            pltpu.VMEM((pieces, CORES, nx, band, width), F32),
            pltpu.VMEM((sups, nx, share, width), F32),
            pltpu.VMEM((pieces, nx, band, width), F32),
            pltpu.VMEM((sups, nx - 1, share, width), F32),
            pltpu.VMEM((pieces, nx - 1, band, width), F32),
            pltpu.VMEM((pieces, band, width), F32),
            pltpu.VMEM((pieces, band, width), F32),
            pltpu.VMEM((sups, rows_local, width), BF16),
            pltpu.VMEM((sups, rows_local, width), BF16),
            dma(q, sups, PARTS), dma(q, sups, PARTS), dma(q, sups, PARTS),
            dma(sups), dma(sups), dma(pieces), dma(pieces),
            dma(sups, nx - 1), dma(sups, nx - 1), dma(pieces, nx - 1), dma(pieces, nx - 1),
            dma(pieces), dma(pieces), dma(pieces), dma(pieces),
        ],
        compiler_params=pltpu.CompilerParams(
            collective_id=0, has_side_effects=True, vmem_limit_bytes=56 * 1024 * 1024
        ),
    )(ancestors, panel, coupling, pivots, tile_lists)


def solution(mesh):
    placed = (
        P(("pole", "row"), "col"),
        P(None, ("pole", "row"), None),
        P("pole", None, None),
        P("pole", None, None),
        P(),
    )
    return jax.shard_map(
        functools.partial(shards, mesh.shape["row"], mesh.shape["col"]),
        mesh=mesh,
        in_specs=placed,
        out_specs=(
            P(None, ("pole", "row", "col"), None),
            P("pole", "col", None),
            P("pole", "col", None),
        ),
        check_vma=False,
    )
```
